32 devices in a mesh: groups: 2 (over y), ex: 8 (over z, x), wid: 2 (over core).
Axes of the slice: x: 2, y: 2, z: 4, core: 2. Of those that a mesh axis runs over, the one named last changes fastest.
Arguments:
- train_sketch: bfloat16 [2048, 65536], P(('groups', 'ex'), 'wid'), parts along dimension 0, may hold values from -6 to 6
- query_sketch: bfloat16 [512, 65536], P(('groups', 'ex'), 'wid'), parts along dimension 0, may hold values from -6 to 6
- sign_bits: int32 [65536], P('wid'), may hold values from 0 to 1
- column_order: int32 [8192], replicated, may hold values from 0 to 8191, each once
- pair_blocks: int32 [32, 2], P('groups'), parts along dimension 0, may hold values from 0 to 15, as said below
Outputs:
- scores: float32 [2048, 32], P(('groups', 'ex')), parts along dimension 0
The draws below stay inside these ranges and needn't reach their ends.
There are 2 independent parts, one for each index of `groups`. The reference program is written for one: setup_inputs(seed, part) draws one part's arguments, and reference() takes and returns one part's arrays. A program takes and returns all parts, laid end to end along the dimension named above; an argument that names none is the same for every part. Nothing has to cross between parts.
Inputs may be any that keep to these rules, and one draw needn't show every extreme that they name: `pair_blocks`: the 4 blocks named by the train blocks a 2 to (a + 1) * 2 - 1 for any a lie in distinct aligned runs of 2 query blocks.
All inputs are finite; a program needn't handle non-finite values.
Results may differ from the reference program's by a relative error of at most 0.0041.
Values may be sent and summed in bfloat16 or wider, within the bound.
A program may use at most 128 MiB of HBM per device.

```python
import math
import jax
import jax.numpy as jnp
from jax import lax

WIDTH = 65536
PROJ = 8192
HBLOCK = 512
TB_DEV = 2
QBLK = 16
QB_DEV = 2
TBLK = 64
TRAIN = 1024
QUERY = 256
NTB = 16
NQB = 16
SLOTS = 2


def draw_pair_blocks(key, part):
    device_list = NQB // QB_DEV
    picks = TB_DEV * SLOTS
    popularity = jax.random.randint(jax.random.fold_in(key, 7), (device_list,), 0, 4)
    popular_boost = jnp.where(popularity == 0, 65536, 0)

    def per_device(device_id):
        device_key = jax.random.fold_in(key, device_id + 11)
        noise_values = jax.random.randint(jax.random.fold_in(device_key, 1), (device_list,), 0, 65536)
        value_entries = (noise_values + popular_boost) * device_list + jnp.arange(device_list, dtype=jnp.int32)
        ranking = jnp.argsort(-value_entries)
        chosen = ranking[:picks].astype(jnp.int32)
        within = jax.random.randint(jax.random.fold_in(device_key, 2), (picks,), 0, QB_DEV)
        return (chosen * QB_DEV + within).astype(jnp.int32)
    pair_rows = jax.vmap(per_device)(jnp.arange(device_list, dtype=jnp.int32))
    return pair_rows.reshape(device_list * TB_DEV, SLOTS)


def touch_ends(values, own_key, low, largest):
    longest = values.shape.index(max(values.shape))
    spots = []
    for shift in (0, 1):
        where = [jax.random.randint(jax.random.fold_in(own_key, axis), (), 0, length) for axis, length in enumerate(values.shape)]
        where[longest] = (where[longest] + shift) % values.shape[longest]
        spots.append(tuple(where))
    return values.at[spots[0]].set(low).at[spots[1]].set(largest)


def steps_of(key, shape, pieces, least, largest):
    factor_of, own = 1.0, jax.random.fold_in(key, 6)
    for dim, blocks in pieces:
        steps = jnp.exp(jax.random.uniform(jax.random.fold_in(own, dim), (blocks,), jnp.float32, least / len(pieces), largest / len(pieces)))
        factor_of = factor_of * jnp.repeat(steps, shape[dim] // blocks).reshape([-1 if axis == dim else 1 for axis in range(len(shape))])
    return factor_of


def bell_draw(key, dims, deviation, most, pieces=(), kind=jnp.bfloat16):
    array = deviation * jax.random.normal(key, dims, jnp.float32)
    if pieces:
        array = array * steps_of(key, dims, pieces, -0.22, 0.18)
    return jnp.clip(array, -most, most).astype(kind)


def setup_inputs(seed: int = 0, part: int = 0) -> dict:
    seeds = jax.random.split(jax.random.key(seed), 6)
    part_splits = jax.random.split(jax.random.fold_in(seeds[5], part), 6)
    train_sketch = bell_draw(part_splits[0], (TRAIN, WIDTH), 1.0, 6.0, ((0, 8), (1, 2)))
    query_sketch = bell_draw(part_splits[1], (QUERY, WIDTH), 1.0, 6.0, ((0, 8), (1, 2)))
    sign_bits = touch_ends(jax.random.randint(seeds[2], (WIDTH,), 0, 2), jax.random.fold_in(seeds[2], 1), 0, 1).astype(jnp.int32)
    column_order = jax.random.permutation(seeds[3], PROJ).astype(jnp.int32)
    pair_blocks = draw_pair_blocks(jax.random.fold_in(jax.random.fold_in(seeds[5], part), 71), part)
    return dict(train_sketch=train_sketch, query_sketch=query_sketch, sign_bits=sign_bits, column_order=column_order, pair_blocks=pair_blocks)


def project_all(sketch_matrix, sign_vals, column_order, row_block):
    scale = 1.0 / math.sqrt(HBLOCK * (WIDTH // PROJ))

    def one_block(block_rows):
        row_count = block_rows.shape[0]
        rotated = (block_rows.astype(jnp.float32) * sign_vals[None, :]).reshape(row_count, WIDTH // HBLOCK, HBLOCK)
        stride_len = 1
        while stride_len < HBLOCK:
            shaped = rotated.reshape(row_count, WIDTH // HBLOCK, HBLOCK // (2 * stride_len), 2, stride_len)
            first_half = shaped[:, :, :, 0, :]
            second_half = shaped[:, :, :, 1, :]
            rotated = jnp.stack([first_half + second_half, first_half - second_half], axis=3).reshape(row_count, WIDTH // HBLOCK, HBLOCK)
            stride_len = stride_len * 2
        segments = rotated.reshape(row_count, WIDTH // PROJ // 2, 2, PROJ)
        even_sum = segments[:, :, 0, :].sum(axis=1)
        odd_sum = segments[:, :, 1, :].sum(axis=1)
        folded = (even_sum + jnp.take(odd_sum, column_order, axis=1)) * scale
        return folded.astype(jnp.bfloat16)
    shaped_rows = sketch_matrix.reshape(-1, row_block, WIDTH)
    projected = lax.map(one_block, shaped_rows)
    return projected.reshape(-1, PROJ)

def reference(train_sketch, query_sketch, sign_bits, column_order, pair_blocks):
    sign_vals = (2 * sign_bits - 1).astype(jnp.float32)
    train_proj = project_all(train_sketch, sign_vals, column_order, TBLK)
    query_proj = project_all(query_sketch, sign_vals, column_order, QBLK)
    train_blocks = train_proj.reshape(NTB, TBLK, PROJ)
    query_blocks = query_proj.reshape(NQB, QBLK, PROJ)

    def tile_row(inputs):
        block_rows, named_blocks = inputs
        gathered_rows = query_blocks[named_blocks.astype(jnp.int32)]
        tiles = jnp.einsum('xk,sck->xsc', block_rows.astype(jnp.float32), gathered_rows.astype(jnp.float32))
        return tiles.reshape(TBLK, SLOTS * QBLK)
    score_tiles = lax.map(tile_row, (train_blocks, pair_blocks))
    return score_tiles.reshape(TRAIN, SLOTS * QBLK) * (1.0 / math.sqrt(PROJ))
```

```python
import functools
import math

import jax
import jax.numpy as jnp
import numpy as np
from jax import lax
from jax.experimental import pallas as pl
from jax.experimental.pallas import tpu as pltpu
from jax.sharding import PartitionSpec as P

WIDTH = 65536
PROJ = 8192
HBLOCK = 512
TB_DEV = 2
QBLK = 16
TBLK = 64
STEP = 1024
MESH = pl.DeviceIdType.MESH


def hadamard_table(order_size):
    table = np.ones((1, 1), np.float32)
    while table.shape[0] < order_size:
        table = np.block([[table, table], [table, -table]])
    return table.astype(jnp.bfloat16)


def fold_kernel(seg_count, half, *refs):
    order_ref, had_ref = refs[0], refs[1]
    train_refs = refs[2:2 + seg_count]
    query_refs = refs[2 + seg_count:2 + 2 * seg_count]
    sign_refs = refs[2 + 2 * seg_count:2 + 3 * seg_count]
    query_out, train_out, even_t, even_q, odd_t, odd_q = refs[2 + 3 * seg_count:]
    step = pl.program_id(0)
    train_rows = train_out.shape[1]
    query_rows = query_out.shape[1]
    hadamard = had_ref[...]
    for sub in range(STEP // HBLOCK):
        cols = pl.ds(sub * HBLOCK, HBLOCK)
        sums = [None, None]
        for seg in range(seg_count):
            signs = sign_refs[seg][:, cols]
            rows = jnp.concatenate([train_refs[seg][:, cols], query_refs[seg][:, cols]], axis=0)
            term = lax.dot_general(
                hadamard, rows * signs, (((1,), (1,)), ((), ())), preferred_element_type=jnp.float32
            )
            sums[seg % 2] = term if sums[seg % 2] is None else sums[seg % 2] + term
        place = pl.ds(pl.multiple_of(step * STEP + sub * HBLOCK, HBLOCK), HBLOCK)
        even_t[place, :] = sums[0][:, :train_rows]
        even_q[place, :query_rows] = sums[0][:, train_rows:]
        odd_t[place, :] = sums[1][:, :train_rows]
        odd_q[place, :query_rows] = sums[1][:, train_rows:]

    @pl.when(step == pl.num_programs(0) - 1)
    def _():
        @pl.loop(0, PROJ // 32)
        def _(group):
            first = pl.multiple_of(group * 32, 32)
            for part in range(4):
                start = pl.multiple_of(first + part * 8, 8)
                places = [order_ref[start + row] for row in range(8)]
                here = pl.ds(start, 8)
                even_t[here, :] += jnp.concatenate([odd_t[pl.ds(at, 1), :] for at in places], axis=0)
                even_q[here, :] += jnp.concatenate([odd_q[pl.ds(at, 1), :] for at in places], axis=0)

        for side in range(2):
            @pl.loop(0, half // HBLOCK)
            def _(block):
                cols = pl.ds(pl.multiple_of(block * HBLOCK, HBLOCK), HBLOCK)
                rows = pl.ds(pl.multiple_of(side * half + block * HBLOCK, HBLOCK), HBLOCK)
                train_out[side, :, cols] = even_t[rows, :].T
                query_out[side, :, cols] = even_q[rows, :].T[:query_rows, :]


def fold_rows(train_sketch, query_sketch, sign_vals, column_order, hadamard):
    train_rows, local_width = train_sketch.shape
    query_rows = query_sketch.shape[0]
    seg_count = local_width // PROJ
    half = PROJ // 2
    steps = PROJ // STEP

    def pieces(rows):
        return [
            pl.BlockSpec((rows, STEP), functools.partial(lambda seg, i: (0, seg * steps + i), seg))
            for seg in range(seg_count)
        ]

    return pl.pallas_call(
        functools.partial(fold_kernel, seg_count, half),
        grid=(steps,),
        out_shape=(
            jax.ShapeDtypeStruct((2, query_rows, half), jnp.float32),
            jax.ShapeDtypeStruct((2, train_rows, half), jnp.float32),
        ),
        in_specs=[
            pl.BlockSpec(memory_space=pltpu.SMEM),
            pl.BlockSpec((HBLOCK, HBLOCK), lambda i: (0, 0)),
            *pieces(train_rows),
            *pieces(query_rows),
            *pieces(1),
        ],
        out_specs=(
            pl.BlockSpec((2, query_rows, half), lambda i: (0, 0, 0)),
            pl.BlockSpec((2, train_rows, half), lambda i: (0, 0, 0)),
        ),
        scratch_shapes=[pltpu.VMEM((PROJ, 128), jnp.float32)] * 4,
        compiler_params=pltpu.CompilerParams(vmem_limit_bytes=48 * 1024 * 1024),
        name="fold_rows",
    )(
        column_order,
        hadamard,
        *[train_sketch] * seg_count,
        *[query_sketch] * seg_count,
        *[sign_vals.reshape(1, local_width)] * seg_count,
    )


def score_kernel(
    outer, inner, query_ref, train_ref, out_ref, query_got, train_got, segment, train_proj, part, part_got,
    wid_send, wid_recv, send_sem, recv_sem,
):
    wid = lax.axis_index("wid")
    other = 1 - wid
    pos = lax.axis_index("ex")
    row, col = pos // inner, lax.rem(pos, inner)
    query_rows = query_ref.shape[1]
    outer_peers = [lax.rem(row + d, outer) for d in range(1, outer)]
    inner_peers = [lax.rem(col + d, inner) for d in range(1, inner)]

    barrier = pltpu.get_barrier_semaphore()
    pl.semaphore_signal(barrier, inc=1, device_id={"wid": other}, device_id_type=MESH)
    for peer in outer_peers:
        pl.semaphore_signal(barrier, inc=1, device_id={"ex": peer * inner + col}, device_id_type=MESH)
    for peer in inner_peers:
        pl.semaphore_signal(barrier, inc=1, device_id={"ex": row * inner + peer}, device_id_type=MESH)
    pl.semaphore_wait(barrier, outer + inner - 1)

    def swap(source, target, index):
        return pltpu.make_async_remote_copy(
            src_ref=source, dst_ref=target, send_sem=wid_send.at[index], recv_sem=wid_recv.at[index],
            device_id={"wid": other}, device_id_type=MESH,
        )

    def slot_rows(slot):
        return segment.at[pl.ds(pl.multiple_of(slot * query_rows, query_rows), query_rows), :]

    def push(slot, target, index):
        return pltpu.make_async_remote_copy(
            src_ref=slot_rows(slot), dst_ref=slot_rows(slot), send_sem=send_sem.at[index],
            recv_sem=recv_sem.at[slot], device_id={"ex": target}, device_id_type=MESH,
        )

    scale = 1.0 / math.sqrt(HBLOCK * (WIDTH // PROJ))
    query_swap = swap(query_ref.at[other], query_got, 0)
    query_swap.start()
    train_swap = swap(train_ref.at[other], train_got, 1)
    query_swap.wait()
    own = pl.ds(pl.multiple_of(pos * query_rows, query_rows), query_rows)
    segment[own, :] = ((query_ref[wid] + query_got[...]) * scale).astype(jnp.bfloat16)
    sent = []

    def send(slot, target):
        copy = push(slot, target, len(sent))
        copy.start()
        sent.append(copy)

    for peer in outer_peers:
        send(pos, peer * inner + col)
    for peer in inner_peers:
        send(pos, row * inner + peer)
    train_swap.start()
    train_swap.wait()
    train_proj[...] = ((train_ref[wid] + train_got[...]) * scale).astype(jnp.bfloat16)
    for d in range(1, outer):
        slot = lax.rem(row + outer - d, outer) * inner + col
        push(slot, pos, 0).wait_recv()
        for peer in inner_peers:
            send(slot, row * inner + peer)
    for d in range(outer):
        for peer in inner_peers:
            push(lax.rem(row + outer - d, outer) * inner + peer, pos, 0).wait_recv()
    width = min(256, part.shape[1])
    for first in range(0, part.shape[1], width):
        part[:, pl.ds(first, width)] = lax.dot_general(
            train_proj[...], segment[pl.ds(first, width), :], (((1,), (1,)), ((), ())),
            preferred_element_type=jnp.float32,
        )
    part_swap = swap(part, part_got, 2)
    part_swap.start()
    part_swap.wait()
    out_ref[...] = (part[...] + part_got[...]) * (1.0 / math.sqrt(PROJ))
    for copy in sent:
        copy.wait_send()


def score_rows(query_part, train_part, ex_count):
    _, query_rows, half = query_part.shape
    train_rows = train_part.shape[1]
    outer = 4 if ex_count % 4 == 0 else 1
    inner = ex_count // outer
    width = ex_count * query_rows
    return pl.pallas_call(
        functools.partial(score_kernel, outer, inner),
        out_shape=jax.ShapeDtypeStruct((train_rows, width), jnp.float32),
        in_specs=[pl.BlockSpec(memory_space=pltpu.VMEM)] * 2,
        out_specs=pl.BlockSpec(memory_space=pltpu.VMEM),
        scratch_shapes=[
            pltpu.VMEM((query_rows, half), jnp.float32),
            pltpu.VMEM((train_rows, half), jnp.float32),
            pltpu.VMEM((width, half), jnp.bfloat16),
            pltpu.VMEM((train_rows, half), jnp.bfloat16),
            pltpu.VMEM((train_rows, width), jnp.float32),
            pltpu.VMEM((train_rows, width), jnp.float32),
            pltpu.SemaphoreType.DMA((3,)),
            pltpu.SemaphoreType.DMA((3,)),
            pltpu.SemaphoreType.DMA((outer - 1 + outer * (inner - 1),)),
            pltpu.SemaphoreType.DMA((ex_count,)),
        ],
        compiler_params=pltpu.CompilerParams(
            collective_id=0, has_side_effects=True, vmem_limit_bytes=48 * 1024 * 1024
        ),
        name="score_rows",
    )(query_part, train_part)


def body(ex_count, train_sketch, query_sketch, sign_bits, column_order, pair_blocks):
    hadamard = jnp.asarray(hadamard_table(HBLOCK))
    sign_vals = (2 * sign_bits - 1).astype(jnp.bfloat16)
    query_part, train_part = fold_rows(train_sketch, query_sketch, sign_vals, column_order, hadamard)
    slot_count = pair_blocks.shape[1]
    device_pos = lax.axis_index("ex")
    local_pairs = lax.dynamic_slice_in_dim(pair_blocks, device_pos * TB_DEV, TB_DEV, 0)
    target_rows = (local_pairs * QBLK)[:, :, None] + jnp.arange(QBLK, dtype=jnp.int32)[None, None, :]
    target_rows = target_rows.reshape(TB_DEV, slot_count * QBLK)
    full_scores = score_rows(query_part, train_part, ex_count)
    seg_rows = full_scores.shape[1]
    row_pos = jnp.arange(seg_rows, dtype=jnp.int32)
    placement = (target_rows[:, :, None] == row_pos[None, None, :]).astype(jnp.float32)
    scores = jnp.einsum(
        "bxr,bcr->bxc",
        full_scores.reshape(TB_DEV, TBLK, seg_rows),
        placement,
        precision=lax.Precision.HIGHEST,
        preferred_element_type=jnp.float32,
    )
    return scores.reshape(TB_DEV * TBLK, slot_count * QBLK)


def solution(mesh):
    placed = (
        P(("groups", "ex"), "wid"),
        P(("groups", "ex"), "wid"),
        P("wid"),
        P(),
        P("groups", None),
    )
    return jax.shard_map(
        functools.partial(body, mesh.shape["ex"]),
        mesh=mesh, in_specs=placed, out_specs=P(("groups", "ex"), None), check_vma=False,
    )
```

```python
import functools
import math

import jax
import jax.numpy as jnp
import numpy as np
from jax import lax
from jax.experimental import pallas as pl
from jax.experimental.pallas import tpu as pltpu
from jax.sharding import PartitionSpec as P

WIDTH = 65536
PROJ = 8192
HBLOCK = 512
TB_DEV = 2
QBLK = 16
TBLK = 64
CHUNK = 16
DOT_ROWS = 512
MESH = pl.DeviceIdType.MESH


def hadamard_table(order_size):
    table = np.ones((1, 1), np.float32)
    while table.shape[0] < order_size:
        table = np.block([[table, table], [table, -table]])
    return table.astype(jnp.bfloat16)


def rotate_group(group, rows, sketch, signs, hadamard, even_part, odd_part):
    half = PROJ // 2
    blocks = DOT_ROWS // rows
    for parity in range(2):
        total = None
        for seg in range(parity, sketch.shape[1] // PROJ, 2):
            pieces = []
            for block in range(blocks):
                start = pl.multiple_of(seg * PROJ + (group * blocks + block) * HBLOCK, HBLOCK)
                cols = pl.ds(start, HBLOCK)
                pieces.append(sketch[:, cols] * signs[:, cols])
            term = jnp.dot(
                jnp.concatenate(pieces, axis=0), hadamard[...], preferred_element_type=jnp.float32
            )
            total = term if total is None else total + term
        for block in range(blocks):
            start = (group * blocks + block) * HBLOCK
            value = total[block * rows:(block + 1) * rows, :]
            if parity == 0:
                side = start // half
                even_part[side, :, pl.ds(pl.multiple_of(start - side * half, HBLOCK), HBLOCK)] = value
            else:
                odd_part[:, pl.ds(pl.multiple_of(start, HBLOCK), HBLOCK)] = value


def turn_odd(rows, odd_part, odd_got, odd_rows):
    @pl.loop(0, PROJ // HBLOCK)
    def _(block):
        span = pl.ds(pl.multiple_of(block * HBLOCK, HBLOCK), HBLOCK)
        odd_rows[span, :rows] = (odd_part[:, span] + odd_got[:, span]).T


def move_rows(base, first, last, order, odd_rows, moved):
    @pl.loop(first // 32, last // 32)
    def _(group):
        for part in range(4):
            start = pl.multiple_of(group * 32 + part * 8, 8)
            places = [order[base + start + row] for row in range(8)]
            moved[pl.ds(start, 8), :] = jnp.concatenate([odd_rows[pl.ds(at, 1), :] for at in places], axis=0)


def fold_half(rows, wid, even_part, even_got, moved, target, target_row):
    scale = 1.0 / math.sqrt(HBLOCK * (WIDTH // PROJ))

    @pl.loop(0, PROJ // 2 // HBLOCK)
    def _(block):
        span = pl.ds(pl.multiple_of(block * HBLOCK, HBLOCK), HBLOCK)
        total = even_part[wid, :, span] + even_got[:, span] + moved[span, :].T[:rows, :]
        target[pl.ds(target_row, rows), span] = (total * scale).astype(jnp.bfloat16)


def score_kernel(
    outer, inner, order, hadamard, signs, query_hbm, train_hbm, out_ref,
    query_in, train_in, query_even, query_odd, query_even_got, query_odd_got,
    train_even, train_odd, train_even_got, train_odd_got, odd_rows, moved,
    segment, train_proj, part, part_got,
    load_sem, wid_send, wid_recv, up_sem, down_sem, inner_sem, recv_sem,
):
    wid = lax.axis_index("wid")
    other = 1 - wid
    pos = lax.axis_index("ex")
    row, col = pos // inner, lax.rem(pos, inner)
    query_rows, train_rows = query_in.shape[0], train_in.shape[0]
    half = PROJ // 2
    chunks = query_rows // CHUNK
    outer_peers = [lax.rem(row + d, outer) for d in range(1, outer)]
    inner_peers = [lax.rem(col + d, inner) for d in range(1, inner)]

    load_query = pltpu.make_async_copy(query_hbm, query_in, load_sem.at[0])
    load_train = pltpu.make_async_copy(train_hbm, train_in, load_sem.at[1])
    load_query.start()
    load_train.start()
    barrier = pltpu.get_barrier_semaphore()
    pl.semaphore_signal(barrier, inc=1, device_id={"wid": other}, device_id_type=MESH)
    for peer in outer_peers:
        pl.semaphore_signal(barrier, inc=1, device_id={"ex": peer * inner + col}, device_id_type=MESH)
    for peer in inner_peers:
        pl.semaphore_signal(barrier, inc=1, device_id={"ex": row * inner + peer}, device_id_type=MESH)

    def swap(source, target, index):
        return pltpu.make_async_remote_copy(
            src_ref=source, dst_ref=target, send_sem=wid_send.at[index], recv_sem=wid_recv.at[index],
            device_id={"wid": other}, device_id_type=MESH,
        )

    def push(slot, chunk, target, sem):
        rows = pl.ds(pl.multiple_of(slot * query_rows + chunk * CHUNK, CHUNK), CHUNK)
        return pltpu.make_async_remote_copy(
            src_ref=segment.at[rows, :], dst_ref=segment.at[rows, :], send_sem=sem,
            recv_sem=recv_sem.at[slot * chunks + chunk], device_id={"ex": target}, device_id_type=MESH,
        )

    def up(step, chunk):
        return push((row - step) * inner + col, chunk, (row + 1) * inner + col, up_sem.at[step * chunks + chunk])

    def down(step, chunk):
        return push((row + step) * inner + col, chunk, (row - 1) * inner + col, down_sem.at[step * chunks + chunk])

    def across(from_row, step, chunk):
        return [
            push(
                from_row * inner + col, chunk, row * inner + peer,
                inner_sem.at[((step + outer - 1) * chunks + chunk) * (inner - 1) + index],
            )
            for index, peer in enumerate(inner_peers)
        ]

    def forward(step, chunk, act):
        @pl.when(row >= step)
        def _():
            if act is run:
                push((row - step) * inner + col, chunk, pos, up_sem.at[0]).wait_recv()

            @pl.when(row < outer - 1)
            def _():
                act(up(step, chunk))

            for copy in across(row - step, -step, chunk):
                act(copy)

        @pl.when(row + step < outer)
        def _():
            if act is run:
                push((row + step) * inner + col, chunk, pos, up_sem.at[0]).wait_recv()

            @pl.when(row > 0)
            def _():
                act(down(step, chunk))

            for copy in across(row + step, step, chunk):
                act(copy)

    def own(chunk, act):
        @pl.when(row < outer - 1)
        def _():
            act(up(0, chunk))

        @pl.when(row > 0)
        def _():
            act(down(0, chunk))

        for copy in across(row, 0, chunk):
            act(copy)

    def run(copy):
        copy.start()

    def finish(copy):
        copy.wait_send()

    load_query.wait()
    for group in range(PROJ // HBLOCK * query_rows // DOT_ROWS):
        rotate_group(group, query_rows, query_in, signs, hadamard, query_even, query_odd)
    pl.semaphore_wait(barrier, outer + inner - 1)
    odd_swap = swap(query_odd, query_odd_got, 0)
    even_swap = swap(query_even.at[other], query_even_got, 1)
    odd_swap.start()
    even_swap.start()
    odd_swap.wait()
    turn_odd(query_rows, query_odd, query_odd_got, odd_rows)
    move_rows(wid * half, 0, half, order, odd_rows, moved)
    even_swap.wait()
    own_row = pl.multiple_of(pos * query_rows, query_rows)
    fold_half(query_rows, wid, query_even, query_even_got, moved, segment, own_row)
    for chunk in range(chunks):
        own(chunk, run)

    train_odd_swap = swap(train_odd, train_odd_got, 2)
    train_even_swap = swap(train_even.at[other], train_even_got, 3)
    groups = PROJ // HBLOCK * train_rows // DOT_ROWS

    def rotate_span(first, last):
        @pl.loop(first, last)
        def _(group):
            rotate_group(group, train_rows, train_in, signs, hadamard, train_even, train_odd)

    def first_part():
        load_train.wait()
        rotate_span(0, groups // 2)

    def second_part():
        rotate_span(groups // 2, groups)
        train_odd_swap.start()
        train_even_swap.start()

    def third_part():
        train_odd_swap.wait()
        turn_odd(train_rows, train_odd, train_odd_got, odd_rows)

    def fourth_part():
        move_rows(wid * half, 0, half // 2, order, odd_rows, moved)

    def fifth_part():
        move_rows(wid * half, half // 2, half, order, odd_rows, moved)

    def sixth_part():
        train_even_swap.wait()
        fold_half(train_rows, wid, train_even, train_even_got, moved, train_proj, 0)

    work = [first_part, second_part, third_part, fourth_part, fifth_part, sixth_part]
    for step in range(1, outer):
        for chunk in range(chunks):
            if work:
                work.pop(0)()
            forward(step, chunk, run)
    for piece in work:
        piece()
    for d in range(outer):
        for peer in inner_peers:
            for chunk in range(chunks):
                push(lax.rem(row + d, outer) * inner + peer, chunk, pos, up_sem.at[0]).wait_recv()
    width = min(256, part.shape[1])
    for first in range(0, part.shape[1], width):
        part[:, pl.ds(first, width)] = lax.dot_general(
            train_proj[...], segment[pl.ds(first, width), :], (((1,), (1,)), ((), ())),
            preferred_element_type=jnp.float32,
        )
    part_swap = swap(part, part_got, 4)
    part_swap.start()
    for chunk in range(chunks):
        own(chunk, finish)
        for step in range(1, outer):
            forward(step, chunk, finish)
    part_swap.wait()
    out_ref[...] = (part[...] + part_got[...]) * (1.0 / math.sqrt(PROJ))


def score_rows(train_sketch, query_sketch, sign_vals, column_order, hadamard, ex_count):
    train_rows, local_width = train_sketch.shape
    query_rows = query_sketch.shape[0]
    half = PROJ // 2
    outer = 4 if ex_count % 4 == 0 else 1
    inner = ex_count // outer
    width = ex_count * query_rows
    chunks = query_rows // CHUNK

    def swapped(rows):
        return [
            pltpu.VMEM((2, rows, half), jnp.float32),
            pltpu.VMEM((rows, PROJ), jnp.float32),
            pltpu.VMEM((rows, half), jnp.float32),
            pltpu.VMEM((rows, PROJ), jnp.float32),
        ]

    return pl.pallas_call(
        functools.partial(score_kernel, outer, inner),
        out_shape=jax.ShapeDtypeStruct((train_rows, width), jnp.float32),
        in_specs=[
            pl.BlockSpec(memory_space=pltpu.SMEM),
            pl.BlockSpec(memory_space=pltpu.VMEM),
            pl.BlockSpec(memory_space=pltpu.VMEM),
            pl.BlockSpec(memory_space=pl.ANY),
            pl.BlockSpec(memory_space=pl.ANY),
        ],
        out_specs=pl.BlockSpec(memory_space=pltpu.VMEM),
        scratch_shapes=[
            pltpu.VMEM((query_rows, local_width), jnp.bfloat16),
            pltpu.VMEM((train_rows, local_width), jnp.bfloat16),
            *swapped(query_rows),
            *swapped(train_rows),
            pltpu.VMEM((PROJ, 128), jnp.float32),
            pltpu.VMEM((half, 128), jnp.float32),
            pltpu.VMEM((width, half), jnp.bfloat16),
            pltpu.VMEM((train_rows, half), jnp.bfloat16),
            pltpu.VMEM((train_rows, width), jnp.float32),
            pltpu.VMEM((train_rows, width), jnp.float32),
            pltpu.SemaphoreType.DMA((2,)),
            pltpu.SemaphoreType.DMA((5,)),
            pltpu.SemaphoreType.DMA((5,)),
            pltpu.SemaphoreType.DMA((outer * chunks,)),
            pltpu.SemaphoreType.DMA((outer * chunks,)),
            pltpu.SemaphoreType.DMA((max(1, (2 * outer - 1) * chunks * (inner - 1)),)),
            pltpu.SemaphoreType.DMA((ex_count * chunks,)),
        ],
        compiler_params=pltpu.CompilerParams(
            collective_id=0, has_side_effects=True, vmem_limit_bytes=60 * 1024 * 1024
        ),
        name="score_rows",
    )(column_order, hadamard, sign_vals.reshape(1, local_width), query_sketch, train_sketch)


def body(ex_count, train_sketch, query_sketch, sign_bits, column_order, pair_blocks):
    hadamard = jnp.asarray(hadamard_table(HBLOCK))
    sign_vals = (2 * sign_bits - 1).astype(jnp.bfloat16)
    slot_count = pair_blocks.shape[1]
    device_pos = lax.axis_index("ex")
    local_pairs = lax.dynamic_slice_in_dim(pair_blocks, device_pos * TB_DEV, TB_DEV, 0)
    target_rows = (local_pairs * QBLK)[:, :, None] + jnp.arange(QBLK, dtype=jnp.int32)[None, None, :]
    target_rows = target_rows.reshape(TB_DEV, slot_count * QBLK)
    full_scores = score_rows(train_sketch, query_sketch, sign_vals, column_order, hadamard, ex_count)
    seg_rows = full_scores.shape[1]
    row_pos = jnp.arange(seg_rows, dtype=jnp.int32)
    placement = (target_rows[:, :, None] == row_pos[None, None, :]).astype(jnp.float32)
    scores = jnp.einsum(
        "bxr,bcr->bxc",
        full_scores.reshape(TB_DEV, TBLK, seg_rows),
        placement,
        precision=lax.Precision.HIGHEST,
        preferred_element_type=jnp.float32,
    )
    return scores.reshape(TB_DEV * TBLK, slot_count * QBLK)


def solution(mesh):
    placed = (
        P(("groups", "ex"), "wid"),
        P(("groups", "ex"), "wid"),
        P("wid"),
        P(),
        P("groups", None),
    )
    return jax.shard_map(
        functools.partial(body, mesh.shape["ex"]),
        mesh=mesh, in_specs=placed, out_specs=P(("groups", "ex"), None), check_vma=False,
    )
```

```python
import functools
import math

import jax
import jax.numpy as jnp
import numpy as np
from jax import lax
from jax.experimental import pallas as pl
from jax.experimental.pallas import tpu as pltpu
from jax.sharding import PartitionSpec as P

WIDTH = 65536
PROJ = 8192
HBLOCK = 512
QBLK = 16
TBLK = 64
CHUNKS = 4
DOT_ROWS = 512
MESH = pl.DeviceIdType.MESH


def hadamard_table(order_size):
    table = np.ones((1, 1), np.float32)
    while table.shape[0] < order_size:
        table = np.block([[table, table], [table, -table]])
    return table.astype(jnp.bfloat16)


def rotate_group(group, rows, sketch, signs, hadamard, even_part, odd_part, even_out=None, odd_out=None):
    half = PROJ // 2
    blocks = DOT_ROWS // rows
    for parity in range(2):
        total = None
        for seg in range(parity, sketch.shape[1] // PROJ, 2):
            pieces = []
            for block in range(blocks):
                start = pl.multiple_of(seg * PROJ + (group * blocks + block) * HBLOCK, HBLOCK)
                cols = pl.ds(start, HBLOCK)
                flip = (2 * signs[:, cols] - 1).astype(jnp.float32).astype(jnp.bfloat16)
                pieces.append(sketch[:, cols] * flip)
            term = jnp.dot(
                jnp.concatenate(pieces, axis=0), hadamard[...], preferred_element_type=jnp.float32
            )
            total = term if total is None else total + term
        for block in range(blocks):
            start = (group * blocks + block) * HBLOCK
            value = total[block * rows:(block + 1) * rows, :].astype(even_part.dtype)
            if parity == 0:
                side = start // half
                span = pl.ds(pl.multiple_of(start - side * half, HBLOCK), HBLOCK)
                even_part[side, :, span] = value
                if even_out is not None:
                    even_out[side, :, span] = value.astype(even_out.dtype)
            else:
                span = pl.ds(pl.multiple_of(start, HBLOCK), HBLOCK)
                odd_part[:, span] = value
                if odd_out is not None:
                    odd_out[:, span] = value.astype(odd_out.dtype)


def turn_odd(rows, odd_part, odd_got, odd_rows):
    @pl.loop(0, PROJ // HBLOCK)
    def _(block):
        span = pl.ds(pl.multiple_of(block * HBLOCK, HBLOCK), HBLOCK)
        odd_rows[span, :rows] = (odd_part[:, span] + odd_got[:, span]).T


def move_rows(base, first, last, order, odd_rows, moved):
    @pl.loop(first // 32, last // 32)
    def _(group):
        for part in range(4):
            start = pl.multiple_of(group * 32 + part * 8, 8)
            places = [order[base + start + row] for row in range(8)]
            moved[pl.ds(start, 8), :] = jnp.concatenate([odd_rows[pl.ds(at, 1), :] for at in places], axis=0)


def fold_half(first, last, rows, wid, even_part, even_got, moved, target, target_row):
    scale = 1.0 / math.sqrt(HBLOCK * (WIDTH // PROJ))

    @pl.loop(first // HBLOCK, last // HBLOCK)
    def _(block):
        span = pl.ds(pl.multiple_of(block * HBLOCK, HBLOCK), HBLOCK)
        total = even_part[wid, :, span] + even_got[:, span] + moved[span, :].T[:rows, :]
        target[pl.ds(target_row, rows), span] = (total * scale).astype(jnp.bfloat16)


def score_kernel(
    outer, inner, order, pairs, hadamard, signs, query_hbm, train_hbm, out_ref,
    query_in, train_in, query_even_out, query_odd_out, query_even, query_odd, query_even_got, query_odd_got,
    train_even, train_odd, train_even_got, train_odd_got, odd_rows, moved,
    segment, train_proj, part, picked, picked_got,
    load_sem, wid_send, wid_recv, up_sem, down_sem, inner_sem, recv_sem,
):
    wid = lax.axis_index("wid")
    other = 1 - wid
    pos = lax.axis_index("ex")
    row, col = pos // inner, lax.rem(pos, inner)
    query_rows, train_rows = query_in.shape[0], train_in.shape[0]
    half = PROJ // 2
    chunks = CHUNKS
    piece = half // chunks
    outer_peers = [lax.rem(row + d, outer) for d in range(1, outer)]
    inner_peers = [lax.rem(col + d, inner) for d in range(1, inner)]

    load_query = pltpu.make_async_copy(query_hbm, query_in, load_sem.at[0])
    load_train = pltpu.make_async_copy(train_hbm, train_in, load_sem.at[1])
    load_query.start()
    barrier = pltpu.get_barrier_semaphore()
    pl.semaphore_signal(barrier, inc=1, device_id={"wid": other}, device_id_type=MESH)
    for peer in outer_peers:
        pl.semaphore_signal(barrier, inc=1, device_id={"ex": peer * inner + col}, device_id_type=MESH)
    for peer in inner_peers:
        pl.semaphore_signal(barrier, inc=1, device_id={"ex": row * inner + peer}, device_id_type=MESH)

    def swap(source, target, index):
        return pltpu.make_async_remote_copy(
            src_ref=source, dst_ref=target, send_sem=wid_send.at[index], recv_sem=wid_recv.at[index],
            device_id={"wid": other}, device_id_type=MESH,
        )

    def push(slot, chunk, target, sem):
        rows = pl.ds(pl.multiple_of(slot * query_rows, query_rows), query_rows)
        span = pl.ds(chunk * piece, piece)
        return pltpu.make_async_remote_copy(
            src_ref=segment.at[rows, span], dst_ref=segment.at[rows, span], send_sem=sem,
            recv_sem=recv_sem.at[slot * chunks + chunk], device_id={"ex": target}, device_id_type=MESH,
        )

    def up(step, chunk):
        return push((row - step) * inner + col, chunk, (row + 1) * inner + col, up_sem.at[step * chunks + chunk])

    def down(step, chunk):
        return push((row + step) * inner + col, chunk, (row - 1) * inner + col, down_sem.at[step * chunks + chunk])

    def across(from_row, step, chunk):
        return [
            push(
                from_row * inner + col, chunk, row * inner + peer,
                inner_sem.at[((step + outer - 1) * chunks + chunk) * (inner - 1) + index],
            )
            for index, peer in enumerate(inner_peers)
        ]

    def forward(step, chunk, act):
        @pl.when(row >= step)
        def _():
            if act is run:
                push((row - step) * inner + col, chunk, pos, up_sem.at[0]).wait_recv()

            @pl.when(row < outer - 1)
            def _():
                act(up(step, chunk))

            for copy in across(row - step, -step, chunk):
                act(copy)

        @pl.when(row + step < outer)
        def _():
            if act is run:
                push((row + step) * inner + col, chunk, pos, up_sem.at[0]).wait_recv()

            @pl.when(row > 0)
            def _():
                act(down(step, chunk))

            for copy in across(row + step, step, chunk):
                act(copy)

    def own(chunk, act):
        @pl.when(row < outer - 1)
        def _():
            act(up(0, chunk))

        @pl.when(row > 0)
        def _():
            act(down(0, chunk))

        for copy in across(row, 0, chunk):
            act(copy)

    def run(copy):
        copy.start()

    def finish(copy):
        copy.wait_send()

    load_query.wait()
    load_train.start()
    for group in range(PROJ // HBLOCK * query_rows // DOT_ROWS):
        rotate_group(group, query_rows, query_in, signs, hadamard, query_even, query_odd, query_even_out, query_odd_out)
    pl.semaphore_wait(barrier, outer + inner - 1)
    odd_swap = swap(query_odd_out, query_odd_got, 0)
    even_swap = swap(query_even_out.at[other], query_even_got, 1)
    odd_swap.start()
    even_swap.start()
    odd_swap.wait()
    turn_odd(query_rows, query_odd, query_odd_got, odd_rows)
    even_swap.wait()
    own_row = pl.multiple_of(pos * query_rows, query_rows)
    for chunk in range(chunks):
        first, last = chunk * piece, (chunk + 1) * piece
        move_rows(wid * half, first, last, order, odd_rows, moved)
        fold_half(first, last, query_rows, wid, query_even, query_even_got, moved, segment, own_row)
        own(chunk, run)

    groups = PROJ // HBLOCK * train_rows // DOT_ROWS
    span_of = PROJ // groups
    odd_spans = [pl.ds(group * span_of, span_of) for group in range(groups)]
    train_odd_swaps = [
        swap(train_odd.at[:, span], train_odd_got.at[:, span], 3 + group) for group, span in enumerate(odd_spans)
    ]
    train_even_swap = swap(train_even.at[other], train_even_got, 3 + groups)

    def rotate_part(group):
        if group == 0:
            load_train.wait()
        rotate_group(group, train_rows, train_in, signs, hadamard, train_even, train_odd)
        train_odd_swaps[group].start()
        if group == groups - 1:
            train_even_swap.start()

    def turn_part():
        for copy in train_odd_swaps:
            copy.wait()
        turn_odd(train_rows, train_odd, train_odd_got, odd_rows)

    def move_part(index):
        move_rows(wid * half, index * piece, (index + 1) * piece, order, odd_rows, moved)

    def fold_part():
        train_even_swap.wait()
        fold_half(0, half, train_rows, wid, train_even, train_even_got, moved, train_proj, 0)

    work = [functools.partial(rotate_part, group) for group in range(groups)]
    work += [lambda: None, turn_part]
    work += [functools.partial(move_part, index) for index in range(chunks)]
    work += [fold_part]
    for step in range(1, outer):
        for chunk in range(chunks):
            if work:
                work.pop(0)()
            forward(step, chunk, run)
    for task in work:
        task()
    for d in range(outer):
        for peer in inner_peers:
            for chunk in range(chunks):
                push(lax.rem(row + d, outer) * inner + peer, chunk, pos, up_sem.at[0]).wait_recv()
    width = min(256, segment.shape[0])
    for first in range(0, segment.shape[0], width):
        tile = lax.dot_general(
            segment[pl.ds(first, width), :], train_proj[...], (((1,), (1,)), ((), ())),
            preferred_element_type=jnp.float32,
        )
        part[pl.ds(first // QBLK, width // QBLK)] = tile.reshape(width // QBLK, QBLK, train_rows)
    lanes = lax.broadcasted_iota(jnp.int32, (QBLK, train_rows), 1)
    for slot in range(pairs.shape[1]):
        tile = None
        for block in range(train_rows // TBLK):
            rows = part[pairs[pos * (train_rows // TBLK) + block, slot]]
            tile = rows if tile is None else jnp.where(lanes >= block * TBLK, rows, tile)
        picked[pl.ds(slot * QBLK, QBLK), :] = tile
    picked_swap = swap(picked, picked_got, 2)
    picked_swap.start()
    for chunk in range(chunks):
        own(chunk, finish)
        for step in range(1, outer):
            forward(step, chunk, finish)
    picked_swap.wait()
    out_ref[...] = ((picked[...] + picked_got[...]) * (1.0 / math.sqrt(PROJ)))


def score_rows(train_sketch, query_sketch, sign_bits, column_order, pair_blocks, hadamard, ex_count):
    train_rows, local_width = train_sketch.shape
    query_rows = query_sketch.shape[0]
    half = PROJ // 2
    outer = 4 if ex_count % 4 == 0 else 1
    inner = ex_count // outer
    width = ex_count * query_rows
    chunks = CHUNKS
    out_width = pair_blocks.shape[1] * QBLK
    groups = PROJ // HBLOCK * train_rows // DOT_ROWS

    def swapped(rows, kind):
        return [
            pltpu.VMEM((2, rows, half), jnp.float32),
            pltpu.VMEM((rows, PROJ), jnp.float32),
            pltpu.VMEM((rows, half), kind),
            pltpu.VMEM((rows, PROJ), kind),
        ]

    return pl.pallas_call(
        functools.partial(score_kernel, outer, inner),
        out_shape=jax.ShapeDtypeStruct((out_width, train_rows), jnp.float32),
        in_specs=[
            pl.BlockSpec(memory_space=pltpu.SMEM),
            pl.BlockSpec(memory_space=pltpu.SMEM),
            pl.BlockSpec(memory_space=pltpu.VMEM),
            pl.BlockSpec(memory_space=pltpu.VMEM),
            pl.BlockSpec(memory_space=pl.ANY),
            pl.BlockSpec(memory_space=pl.ANY),
        ],
        out_specs=pl.BlockSpec(memory_space=pltpu.VMEM),
        scratch_shapes=[
            pltpu.VMEM((query_rows, local_width), jnp.bfloat16),
            pltpu.VMEM((train_rows, local_width), jnp.bfloat16),
            pltpu.VMEM((2, query_rows, half), jnp.bfloat16),
            pltpu.VMEM((query_rows, PROJ), jnp.bfloat16),
            *swapped(query_rows, jnp.bfloat16),
            *swapped(train_rows, jnp.float32),
            pltpu.VMEM((PROJ, 128), jnp.float32),
            pltpu.VMEM((half, 128), jnp.float32),
            pltpu.VMEM((width, half), jnp.bfloat16),
            pltpu.VMEM((train_rows, half), jnp.bfloat16),
            pltpu.VMEM((width // QBLK, QBLK, train_rows), jnp.float32),
            pltpu.VMEM((out_width, train_rows), jnp.float32),
            pltpu.VMEM((out_width, train_rows), jnp.float32),
            pltpu.SemaphoreType.DMA((2,)),
            pltpu.SemaphoreType.DMA((4 + groups,)),
            pltpu.SemaphoreType.DMA((4 + groups,)),
            pltpu.SemaphoreType.DMA((outer * chunks,)),
            pltpu.SemaphoreType.DMA((outer * chunks,)),
            pltpu.SemaphoreType.DMA((max(1, (2 * outer - 1) * chunks * (inner - 1)),)),
            pltpu.SemaphoreType.DMA((ex_count * chunks,)),
        ],
        compiler_params=pltpu.CompilerParams(
            collective_id=0, has_side_effects=True, vmem_limit_bytes=60 * 1024 * 1024
        ),
        name="score_rows",
    )(column_order, pair_blocks, hadamard, sign_bits.reshape(1, local_width), query_sketch, train_sketch)


def body(ex_count, train_sketch, query_sketch, sign_bits, column_order, pair_blocks):
    hadamard = jnp.asarray(hadamard_table(HBLOCK))
    return score_rows(train_sketch, query_sketch, sign_bits, column_order, pair_blocks, hadamard, ex_count).T


def solution(mesh):
    placed = (
        P(("groups", "ex"), "wid"),
        P(("groups", "ex"), "wid"),
        P("wid"),
        P(),
        P("groups", None),
    )
    return jax.shard_map(
        functools.partial(body, mesh.shape["ex"]),
        mesh=mesh, in_specs=placed, out_specs=P(("groups", "ex"), None), check_vma=False,
    )
```

```python
import functools
import math

import jax
import jax.numpy as jnp
import numpy as np
from jax import lax
from jax.experimental import pallas as pl
from jax.experimental.pallas import tpu as pltpu
from jax.sharding import PartitionSpec as P

WIDTH = 65536
PROJ = 8192
HBLOCK = 512
QBLK = 16
TBLK = 64
CHUNKS = 4
DOT_ROWS = 512
MESH = pl.DeviceIdType.MESH


def hadamard_table(order_size):
    table = np.ones((1, 1), np.float32)
    while table.shape[0] < order_size:
        table = np.block([[table, table], [table, -table]])
    return table.astype(jnp.bfloat16)


def rotate_group(group, rows, sketch, signs, hadamard, even_part, odd_part, even_out=None, odd_out=None):
    half = PROJ // 2
    blocks = DOT_ROWS // rows
    for parity in range(2):
        total = None
        for seg in range(parity, sketch.shape[1] // PROJ, 2):
            pieces = []
            for block in range(blocks):
                start = pl.multiple_of(seg * PROJ + (group * blocks + block) * HBLOCK, HBLOCK)
                cols = pl.ds(start, HBLOCK)
                flip = (2 * signs[:, cols] - 1).astype(jnp.float32).astype(jnp.bfloat16)
                pieces.append(sketch[:, cols] * flip)
            term = jnp.dot(
                jnp.concatenate(pieces, axis=0), hadamard[...], preferred_element_type=jnp.float32
            )
            total = term if total is None else total + term
        for block in range(blocks):
            start = (group * blocks + block) * HBLOCK
            value = total[block * rows:(block + 1) * rows, :].astype(even_part.dtype)
            if parity == 0:
                side = start // half
                span = pl.ds(pl.multiple_of(start - side * half, HBLOCK), HBLOCK)
                even_part[side, :, span] = value
                if even_out is not None:
                    even_out[side, :, span] = value.astype(even_out.dtype)
            else:
                span = pl.ds(pl.multiple_of(start, HBLOCK), HBLOCK)
                odd_part[:, span] = value
                if odd_out is not None:
                    odd_out[:, span] = value.astype(odd_out.dtype)


def turn_odd(rows, odd_part, odd_got, odd_rows):
    @pl.loop(0, PROJ // HBLOCK)
    def _(block):
        span = pl.ds(pl.multiple_of(block * HBLOCK, HBLOCK), HBLOCK)
        odd_rows[span, :rows] = (odd_part[:, span] + odd_got[:, span]).T


def move_rows(base, first, last, order, odd_rows, moved):
    @pl.loop(first // 32, last // 32)
    def _(group):
        for part in range(4):
            start = pl.multiple_of(group * 32 + part * 8, 8)
            places = [order[base + start + row] for row in range(8)]
            moved[pl.ds(start, 8), :] = jnp.concatenate([odd_rows[pl.ds(at, 1), :] for at in places], axis=0)


def fold_half(first, last, rows, wid, even_part, even_got, moved, target, target_row):
    scale = 1.0 / math.sqrt(HBLOCK * (WIDTH // PROJ))

    @pl.loop(first // HBLOCK, last // HBLOCK)
    def _(block):
        span = pl.ds(pl.multiple_of(block * HBLOCK, HBLOCK), HBLOCK)
        total = even_part[wid, :, span] + even_got[:, span] + moved[span, :].T[:rows, :]
        target[pl.ds(target_row, rows), span] = (total * scale).astype(jnp.bfloat16)


def score_kernel(
    outer, inner, order, pairs, hadamard, signs, query_hbm, train_hbm, out_ref,
    query_in, train_in, query_even_out, query_odd_out, query_even, query_odd, query_even_got, query_odd_got,
    train_even, train_odd, train_even_got, train_odd_got, odd_rows, moved,
    segment, train_proj, part, picked, picked_got,
    load_sem, wid_send, wid_recv, up_sem, down_sem, relay_sem, inner_sem, recv_sem,
):
    wid = lax.axis_index("wid")
    other = 1 - wid
    pos = lax.axis_index("ex")
    row, col = pos // inner, lax.rem(pos, inner)
    query_rows, train_rows = query_in.shape[0], train_in.shape[0]
    half = PROJ // 2
    chunks = CHUNKS
    piece = half // chunks
    outer_peers = [lax.rem(row + d, outer) for d in range(1, outer)]
    inner_peers = [lax.rem(col + d, inner) for d in range(1, inner)]
    shared = chunks // 2 if inner == 2 and outer == 4 else 0

    load_query = pltpu.make_async_copy(query_hbm, query_in, load_sem.at[0])
    load_train = pltpu.make_async_copy(train_hbm, train_in, load_sem.at[1])
    load_query.start()
    barrier = pltpu.get_barrier_semaphore()
    pl.semaphore_signal(barrier, inc=1, device_id={"wid": other}, device_id_type=MESH)
    for peer in outer_peers:
        pl.semaphore_signal(barrier, inc=1, device_id={"ex": peer * inner + col}, device_id_type=MESH)
    for peer in inner_peers:
        pl.semaphore_signal(barrier, inc=1, device_id={"ex": row * inner + peer}, device_id_type=MESH)

    def swap(source, target, index):
        return pltpu.make_async_remote_copy(
            src_ref=source, dst_ref=target, send_sem=wid_send.at[index], recv_sem=wid_recv.at[index],
            device_id={"wid": other}, device_id_type=MESH,
        )

    def push(slot, chunk, target, sem):
        rows = pl.ds(pl.multiple_of(slot * query_rows, query_rows), query_rows)
        span = pl.ds(chunk * piece, piece)
        return pltpu.make_async_remote_copy(
            src_ref=segment.at[rows, span], dst_ref=segment.at[rows, span], send_sem=sem,
            recv_sem=recv_sem.at[slot * chunks + chunk], device_id={"ex": target}, device_id_type=MESH,
        )

    def up(step, chunk):
        return push((row - step) * inner + col, chunk, (row + 1) * inner + col, up_sem.at[step * chunks + chunk])

    def down(step, chunk):
        return push((row + step) * inner + col, chunk, (row - 1) * inner + col, down_sem.at[step * chunks + chunk])

    def across(from_row, step, chunk):
        return [
            push(
                from_row * inner + col, chunk, row * inner + peer,
                inner_sem.at[((step + outer - 1) * chunks + chunk) * (inner - 1) + index],
            )
            for index, peer in enumerate(inner_peers)
        ]

    def forward(step, chunk, act):
        @pl.when(row >= step)
        def _():
            if act is run:
                push((row - step) * inner + col, chunk, pos, up_sem.at[0]).wait_recv()

            @pl.when(row < outer - 1)
            def _():
                act(up(step, chunk))

            @pl.when((row > step) if chunk < shared else (row >= step))
            def _():
                for copy in across(row - step, -step, chunk):
                    act(copy)

        @pl.when(row + step < outer)
        def _():
            if act is run:
                push((row + step) * inner + col, chunk, pos, up_sem.at[0]).wait_recv()

            @pl.when(row > 0)
            def _():
                act(down(step, chunk))

            @pl.when((row + step < outer - 1) if chunk < shared else (row + step < outer))
            def _():
                for copy in across(row + step, step, chunk):
                    act(copy)

    def relay(step, chunk, act):
        @pl.when(row == step)
        def _():
            slot = inner_peers[0]
            if act is run:
                push(slot, chunk, pos, up_sem.at[0]).wait_recv()

            @pl.when(row < outer - 1)
            def _():
                act(push(slot, chunk, (row + 1) * inner + col, relay_sem.at[chunk]))

        @pl.when(row + step == outer - 1)
        def _():
            slot = (outer - 1) * inner + inner_peers[0]
            if act is run:
                push(slot, chunk, pos, up_sem.at[0]).wait_recv()

            @pl.when(row > 0)
            def _():
                act(push(slot, chunk, (row - 1) * inner + col, relay_sem.at[chunks + chunk]))

    def own(chunk, act):
        @pl.when(row < outer - 1)
        def _():
            act(up(0, chunk))

        @pl.when(row > 0)
        def _():
            act(down(0, chunk))

        for copy in across(row, 0, chunk):
            act(copy)

    def run(copy):
        copy.start()

    def finish(copy):
        copy.wait_send()

    load_query.wait()
    load_train.start()
    for group in range(PROJ // HBLOCK * query_rows // DOT_ROWS):
        rotate_group(group, query_rows, query_in, signs, hadamard, query_even, query_odd, query_even_out, query_odd_out)
    pl.semaphore_wait(barrier, outer + inner - 1)
    odd_swap = swap(query_odd_out, query_odd_got, 0)
    even_swap = swap(query_even_out.at[other], query_even_got, 1)
    odd_swap.start()
    even_swap.start()
    odd_swap.wait()
    turn_odd(query_rows, query_odd, query_odd_got, odd_rows)
    even_swap.wait()
    own_row = pl.multiple_of(pos * query_rows, query_rows)
    for chunk in range(chunks):
        first, last = chunk * piece, (chunk + 1) * piece
        move_rows(wid * half, first, last, order, odd_rows, moved)
        fold_half(first, last, query_rows, wid, query_even, query_even_got, moved, segment, own_row)
        own(chunk, run)

    groups = PROJ // HBLOCK * train_rows // DOT_ROWS
    span_of = PROJ // groups
    odd_spans = [pl.ds(group * span_of, span_of) for group in range(groups)]
    train_odd_swaps = [
        swap(train_odd.at[:, span], train_odd_got.at[:, span], 3 + group) for group, span in enumerate(odd_spans)
    ]
    train_even_swap = swap(train_even.at[other], train_even_got, 3 + groups)

    def rotate_part(group):
        if group == 0:
            load_train.wait()
        rotate_group(group, train_rows, train_in, signs, hadamard, train_even, train_odd)
        train_odd_swaps[group].start()
        if group == groups - 1:
            train_even_swap.start()

    def turn_part():
        for copy in train_odd_swaps:
            copy.wait()
        turn_odd(train_rows, train_odd, train_odd_got, odd_rows)

    def move_part(index):
        move_rows(wid * half, index * piece, (index + 1) * piece, order, odd_rows, moved)

    def fold_part():
        train_even_swap.wait()
        fold_half(0, half, train_rows, wid, train_even, train_even_got, moved, train_proj, 0)

    work = [functools.partial(rotate_part, group) for group in range(groups)]
    work += [lambda: None, turn_part]
    work += [functools.partial(move_part, index) for index in range(chunks)]
    work += [fold_part]
    work.pop(0)()
    for chunk in range(shared):
        relay(0, chunk, run)
    for step in range(1, outer):
        for chunk in range(chunks):
            if work:
                work.pop(0)()
            forward(step, chunk, run)
        for chunk in range(shared):
            relay(step, chunk, run)
    for task in work:
        task()
    for from_row in range(outer):
        for peer in inner_peers:
            for chunk in range(shared if from_row in (0, outer - 1) else 0, chunks):
                push(from_row * inner + peer, chunk, pos, up_sem.at[0]).wait_recv()
    width = min(256, segment.shape[0])
    for first in range(0, segment.shape[0], width):
        tile = lax.dot_general(
            segment[pl.ds(first, width), :], train_proj[...], (((1,), (1,)), ((), ())),
            preferred_element_type=jnp.float32,
        )
        part[pl.ds(first // QBLK, width // QBLK)] = tile.reshape(width // QBLK, QBLK, train_rows)
    lanes = lax.broadcasted_iota(jnp.int32, (QBLK, train_rows), 1)
    for slot in range(pairs.shape[0]):
        tile = None
        for block in range(train_rows // TBLK):
            rows = part[pairs[slot, pos * (train_rows // TBLK) + block]]
            tile = rows if tile is None else jnp.where(lanes >= block * TBLK, rows, tile)
        picked[pl.ds(slot * QBLK, QBLK), :] = tile
    picked_swap = swap(picked, picked_got, 2)
    picked_swap.start()
    for chunk in range(chunks):
        own(chunk, finish)
        for step in range(1, outer):
            forward(step, chunk, finish)
    for step in range(outer):
        for chunk in range(shared):
            relay(step, chunk, finish)
    picked_swap.wait()
    out_ref[...] = ((picked[...] + picked_got[...]) * (1.0 / math.sqrt(PROJ)))


def score_rows(train_sketch, query_sketch, sign_bits, column_order, pair_blocks, hadamard, ex_count):
    train_rows, local_width = train_sketch.shape
    query_rows = query_sketch.shape[0]
    half = PROJ // 2
    outer = 4 if ex_count % 4 == 0 else 1
    inner = ex_count // outer
    width = ex_count * query_rows
    chunks = CHUNKS
    out_width = pair_blocks.shape[1] * QBLK
    groups = PROJ // HBLOCK * train_rows // DOT_ROWS

    def swapped(rows, kind):
        return [
            pltpu.VMEM((2, rows, half), jnp.float32),
            pltpu.VMEM((rows, PROJ), jnp.float32),
            pltpu.VMEM((rows, half), kind),
            pltpu.VMEM((rows, PROJ), kind),
        ]

    return pl.pallas_call(
        functools.partial(score_kernel, outer, inner),
        out_shape=jax.ShapeDtypeStruct((out_width, train_rows), jnp.float32),
        in_specs=[
            pl.BlockSpec(memory_space=pltpu.SMEM),
            pl.BlockSpec(memory_space=pltpu.SMEM),
            pl.BlockSpec(memory_space=pltpu.VMEM),
            pl.BlockSpec(memory_space=pltpu.VMEM),
            pl.BlockSpec(memory_space=pl.ANY),
            pl.BlockSpec(memory_space=pl.ANY),
        ],
        out_specs=pl.BlockSpec(memory_space=pltpu.VMEM),
        scratch_shapes=[
            pltpu.VMEM((query_rows, local_width), jnp.bfloat16),
            pltpu.VMEM((train_rows, local_width), jnp.bfloat16),
            pltpu.VMEM((2, query_rows, half), jnp.bfloat16),
            pltpu.VMEM((query_rows, PROJ), jnp.bfloat16),
            *swapped(query_rows, jnp.bfloat16),
            *swapped(train_rows, jnp.float32),
            pltpu.VMEM((PROJ, 128), jnp.float32),
            pltpu.VMEM((half, 128), jnp.float32),
            pltpu.VMEM((width, half), jnp.bfloat16),
            pltpu.VMEM((train_rows, half), jnp.bfloat16),
            pltpu.VMEM((width // QBLK, QBLK, train_rows), jnp.float32),
            pltpu.VMEM((out_width, train_rows), jnp.float32),
            pltpu.VMEM((out_width, train_rows), jnp.float32),
            pltpu.SemaphoreType.DMA((2,)),
            pltpu.SemaphoreType.DMA((4 + groups,)),
            pltpu.SemaphoreType.DMA((4 + groups,)),
            pltpu.SemaphoreType.DMA((outer * chunks,)),
            pltpu.SemaphoreType.DMA((outer * chunks,)),
            pltpu.SemaphoreType.DMA((2 * chunks,)),
            pltpu.SemaphoreType.DMA((max(1, (2 * outer - 1) * chunks * (inner - 1)),)),
            pltpu.SemaphoreType.DMA((ex_count * chunks,)),
        ],
        compiler_params=pltpu.CompilerParams(
            collective_id=0, has_side_effects=True, vmem_limit_bytes=60 * 1024 * 1024
        ),
        name="score_rows",
    )(column_order, pair_blocks.T, hadamard, sign_bits.reshape(1, local_width), query_sketch, train_sketch)


def body(ex_count, train_sketch, query_sketch, sign_bits, column_order, pair_blocks):
    hadamard = jnp.asarray(hadamard_table(HBLOCK))
    return score_rows(train_sketch, query_sketch, sign_bits, column_order, pair_blocks, hadamard, ex_count).T


def solution(mesh):
    placed = (
        P(("groups", "ex"), "wid"),
        P(("groups", "ex"), "wid"),
        P("wid"),
        P(),
        P("groups", None),
    )
    return jax.shard_map(
        functools.partial(body, mesh.shape["ex"]),
        mesh=mesh, in_specs=placed, out_specs=P(("groups", "ex"), None), check_vma=False,
    )
```

```python
import functools
import math

import jax
import jax.numpy as jnp
import numpy as np
from jax import lax
from jax.experimental import pallas as pl
from jax.experimental.pallas import tpu as pltpu
from jax.sharding import PartitionSpec as P

WIDTH = 65536
PROJ = 8192
HBLOCK = 512
QBLK = 16
TBLK = 64
CHUNKS = 4
DOT_ROWS = 512
MESH = pl.DeviceIdType.MESH


def hadamard_table(order_size):
    table = np.ones((1, 1), np.float32)
    while table.shape[0] < order_size:
        table = np.block([[table, table], [table, -table]])
    return table.astype(jnp.bfloat16)


def rotate_group(group, rows, sketch, signs, hadamard, even_part, odd_part, even_out=None, odd_out=None, parities=(0, 1)):
    half = PROJ // 2
    blocks = DOT_ROWS // rows
    for parity in parities:
        total = None
        for seg in range(parity, sketch.shape[1] // PROJ, 2):
            pieces = []
            for block in range(blocks):
                start = pl.multiple_of(seg * PROJ + (group * blocks + block) * HBLOCK, HBLOCK)
                cols = pl.ds(start, HBLOCK)
                flip = (2 * signs[:, cols] - 1).astype(jnp.float32).astype(jnp.bfloat16)
                pieces.append(sketch[:, cols] * flip)
            term = jnp.dot(
                jnp.concatenate(pieces, axis=0), hadamard[...], preferred_element_type=jnp.float32
            )
            total = term if total is None else total + term
        for block in range(blocks):
            start = (group * blocks + block) * HBLOCK
            value = total[block * rows:(block + 1) * rows, :].astype(even_part.dtype)
            if parity == 0:
                side = start // half
                span = pl.ds(pl.multiple_of(start - side * half, HBLOCK), HBLOCK)
                even_part[side, :, span] = value
                if even_out is not None:
                    even_out[side, :, span] = value.astype(even_out.dtype)
            else:
                span = pl.ds(pl.multiple_of(start, HBLOCK), HBLOCK)
                odd_part[:, span] = value
                if odd_out is not None:
                    odd_out[:, span] = value.astype(odd_out.dtype)


def turn_odd(rows, odd_part, odd_got, odd_rows):
    @pl.loop(0, PROJ // HBLOCK)
    def _(block):
        span = pl.ds(pl.multiple_of(block * HBLOCK, HBLOCK), HBLOCK)
        odd_rows[span, :rows] = (odd_part[:, span] + odd_got[:, span]).T


def move_rows(base, first, last, order, odd_rows, moved):
    @pl.loop(first // 32, last // 32)
    def _(group):
        for part in range(4):
            start = pl.multiple_of(group * 32 + part * 8, 8)
            places = [order[base + start + row] for row in range(8)]
            moved[pl.ds(start, 8), :] = jnp.concatenate([odd_rows[pl.ds(at, 1), :] for at in places], axis=0)


def fold_half(first, last, rows, wid, even_part, even_got, moved, target, target_row):
    scale = 1.0 / math.sqrt(HBLOCK * (WIDTH // PROJ))

    @pl.loop(first // HBLOCK, last // HBLOCK)
    def _(block):
        span = pl.ds(pl.multiple_of(block * HBLOCK, HBLOCK), HBLOCK)
        total = even_part[wid, :, span] + even_got[:, span] + moved[span, :].T[:rows, :]
        target[pl.ds(target_row, rows), span] = (total * scale).astype(jnp.bfloat16)


def score_kernel(
    outer, inner, order, pairs, hadamard, signs, query_hbm, train_hbm, out_ref,
    query_in, train_in, query_even_out, query_odd_out, query_even, query_odd, query_even_got, query_odd_got,
    train_even, train_odd, train_even_got, train_odd_got, odd_rows, moved,
    segment, train_proj, part, picked, picked_got,
    load_sem, wid_send, wid_recv, up_sem, down_sem, relay_sem, inner_sem, recv_sem,
):
    wid = lax.axis_index("wid")
    other = 1 - wid
    pos = lax.axis_index("ex")
    row, col = pos // inner, lax.rem(pos, inner)
    query_rows, train_rows = query_in.shape[0], train_in.shape[0]
    half = PROJ // 2
    chunks = CHUNKS
    piece = half // chunks
    outer_peers = [lax.rem(row + d, outer) for d in range(1, outer)]
    inner_peers = [lax.rem(col + d, inner) for d in range(1, inner)]
    shared = chunks // 2 if inner == 2 and outer == 4 else 0

    load_query = pltpu.make_async_copy(query_hbm, query_in, load_sem.at[0])
    load_train = pltpu.make_async_copy(train_hbm, train_in, load_sem.at[1])
    load_query.start()
    barrier = pltpu.get_barrier_semaphore()
    pl.semaphore_signal(barrier, inc=1, device_id={"wid": other}, device_id_type=MESH)
    for peer in outer_peers:
        pl.semaphore_signal(barrier, inc=1, device_id={"ex": peer * inner + col}, device_id_type=MESH)
    for peer in inner_peers:
        pl.semaphore_signal(barrier, inc=1, device_id={"ex": row * inner + peer}, device_id_type=MESH)

    def swap(source, target, index):
        return pltpu.make_async_remote_copy(
            src_ref=source, dst_ref=target, send_sem=wid_send.at[index], recv_sem=wid_recv.at[index],
            device_id={"wid": other}, device_id_type=MESH,
        )

    def push(slot, chunk, target, sem):
        rows = pl.ds(pl.multiple_of(slot * query_rows, query_rows), query_rows)
        span = pl.ds(chunk * piece, piece)
        return pltpu.make_async_remote_copy(
            src_ref=segment.at[rows, span], dst_ref=segment.at[rows, span], send_sem=sem,
            recv_sem=recv_sem.at[slot * chunks + chunk], device_id={"ex": target}, device_id_type=MESH,
        )

    def up(step, chunk):
        return push((row - step) * inner + col, chunk, (row + 1) * inner + col, up_sem.at[step * chunks + chunk])

    def down(step, chunk):
        return push((row + step) * inner + col, chunk, (row - 1) * inner + col, down_sem.at[step * chunks + chunk])

    def across(from_row, step, chunk):
        return [
            push(
                from_row * inner + col, chunk, row * inner + peer,
                inner_sem.at[((step + outer - 1) * chunks + chunk) * (inner - 1) + index],
            )
            for index, peer in enumerate(inner_peers)
        ]

    def forward(step, chunk, act):
        @pl.when(row >= step)
        def _():
            if act is run:
                push((row - step) * inner + col, chunk, pos, up_sem.at[0]).wait_recv()

            @pl.when(row < outer - 1)
            def _():
                act(up(step, chunk))

            @pl.when((row > step) if chunk < shared else (row >= step))
            def _():
                for copy in across(row - step, -step, chunk):
                    act(copy)

        @pl.when(row + step < outer)
        def _():
            if act is run:
                push((row + step) * inner + col, chunk, pos, up_sem.at[0]).wait_recv()

            @pl.when(row > 0)
            def _():
                act(down(step, chunk))

            @pl.when((row + step < outer - 1) if chunk < shared else (row + step < outer))
            def _():
                for copy in across(row + step, step, chunk):
                    act(copy)

    def relay(step, chunk, act):
        @pl.when(row == step)
        def _():
            slot = inner_peers[0]
            if act is run:
                push(slot, chunk, pos, up_sem.at[0]).wait_recv()

            @pl.when(row < outer - 1)
            def _():
                act(push(slot, chunk, (row + 1) * inner + col, relay_sem.at[chunk]))

        @pl.when(row + step == outer - 1)
        def _():
            slot = (outer - 1) * inner + inner_peers[0]
            if act is run:
                push(slot, chunk, pos, up_sem.at[0]).wait_recv()

            @pl.when(row > 0)
            def _():
                act(push(slot, chunk, (row - 1) * inner + col, relay_sem.at[chunks + chunk]))

    def own(chunk, act):
        @pl.when(row < outer - 1)
        def _():
            act(up(0, chunk))

        @pl.when(row > 0)
        def _():
            act(down(0, chunk))

        for copy in across(row, 0, chunk):
            act(copy)

    def run(copy):
        copy.start()

    def finish(copy):
        copy.wait_send()

    load_query.wait()
    load_train.start()
    odd_swap = swap(query_odd_out, query_odd_got, 0)
    even_swap = swap(query_even_out.at[other], query_even_got, 1)

    def rotate_query(parity):
        for group in range(PROJ // HBLOCK * query_rows // DOT_ROWS):
            rotate_group(
                group, query_rows, query_in, signs, hadamard, query_even, query_odd, query_even_out, query_odd_out,
                (parity,),
            )

    rotate_query(1)
    pl.semaphore_wait(barrier, outer + inner - 1)
    odd_swap.start()
    rotate_query(0)
    even_swap.start()
    odd_swap.wait()
    turn_odd(query_rows, query_odd, query_odd_got, odd_rows)
    even_swap.wait()
    own_row = pl.multiple_of(pos * query_rows, query_rows)
    for chunk in range(chunks):
        first, last = chunk * piece, (chunk + 1) * piece
        move_rows(wid * half, first, last, order, odd_rows, moved)
        fold_half(first, last, query_rows, wid, query_even, query_even_got, moved, segment, own_row)
        own(chunk, run)

    groups = PROJ // HBLOCK * train_rows // DOT_ROWS
    span_of = PROJ // groups
    odd_spans = [pl.ds(group * span_of, span_of) for group in range(groups)]
    train_odd_swaps = [
        swap(train_odd.at[:, span], train_odd_got.at[:, span], 3 + group) for group, span in enumerate(odd_spans)
    ]
    train_even_swap = swap(train_even.at[other], train_even_got, 3 + groups)

    def rotate_part(group):
        if group == 0:
            load_train.wait()
        rotate_group(group, train_rows, train_in, signs, hadamard, train_even, train_odd)
        train_odd_swaps[group].start()
        if group == groups - 1:
            train_even_swap.start()

    def turn_part():
        for copy in train_odd_swaps:
            copy.wait()
        turn_odd(train_rows, train_odd, train_odd_got, odd_rows)

    def move_part(index):
        move_rows(wid * half, index * piece, (index + 1) * piece, order, odd_rows, moved)

    def fold_part():
        train_even_swap.wait()
        fold_half(0, half, train_rows, wid, train_even, train_even_got, moved, train_proj, 0)

    work = [functools.partial(rotate_part, group) for group in range(groups)]
    work += [lambda: None, turn_part]
    work += [functools.partial(move_part, index) for index in range(chunks)]
    work += [fold_part]
    work.pop(0)()
    for chunk in range(shared):
        relay(0, chunk, run)
    for step in range(1, outer):
        for chunk in range(chunks):
            if work:
                work.pop(0)()
            forward(step, chunk, run)
        for chunk in range(shared):
            relay(step, chunk, run)
    for task in work:
        task()
    for from_row in range(outer):
        for peer in inner_peers:
            for chunk in range(shared if from_row in (0, outer - 1) else 0, chunks):
                push(from_row * inner + peer, chunk, pos, up_sem.at[0]).wait_recv()
    width = min(256, segment.shape[0])
    for first in range(0, segment.shape[0], width):
        tile = lax.dot_general(
            segment[pl.ds(first, width), :], train_proj[...], (((1,), (1,)), ((), ())),
            preferred_element_type=jnp.float32,
        )
        part[pl.ds(first // QBLK, width // QBLK)] = tile.reshape(width // QBLK, QBLK, train_rows)
    lanes = lax.broadcasted_iota(jnp.int32, (QBLK, train_rows), 1)
    for slot in range(pairs.shape[0]):
        tile = None
        for block in range(train_rows // TBLK):
            rows = part[pairs[slot, pos * (train_rows // TBLK) + block]]
            tile = rows if tile is None else jnp.where(lanes >= block * TBLK, rows, tile)
        picked[pl.ds(slot * QBLK, QBLK), :] = tile
    picked_swap = swap(picked, picked_got, 2)
    picked_swap.start()
    for chunk in range(chunks):
        own(chunk, finish)
        for step in range(1, outer):
            forward(step, chunk, finish)
    for step in range(outer):
        for chunk in range(shared):
            relay(step, chunk, finish)
    picked_swap.wait()
    out_ref[...] = ((picked[...] + picked_got[...]) * (1.0 / math.sqrt(PROJ)))


def score_rows(train_sketch, query_sketch, sign_bits, column_order, pair_blocks, hadamard, ex_count):
    train_rows, local_width = train_sketch.shape
    query_rows = query_sketch.shape[0]
    half = PROJ // 2
    outer = 4 if ex_count % 4 == 0 else 1
    inner = ex_count // outer
    width = ex_count * query_rows
    chunks = CHUNKS
    out_width = pair_blocks.shape[1] * QBLK
    groups = PROJ // HBLOCK * train_rows // DOT_ROWS

    def swapped(rows, kind):
        return [
            pltpu.VMEM((2, rows, half), jnp.float32),
            pltpu.VMEM((rows, PROJ), jnp.float32),
            pltpu.VMEM((rows, half), kind),
            pltpu.VMEM((rows, PROJ), kind),
        ]

    return pl.pallas_call(
        functools.partial(score_kernel, outer, inner),
        out_shape=jax.ShapeDtypeStruct((out_width, train_rows), jnp.float32),
        in_specs=[
            pl.BlockSpec(memory_space=pltpu.SMEM),
            pl.BlockSpec(memory_space=pltpu.SMEM),
            pl.BlockSpec(memory_space=pltpu.VMEM),
            pl.BlockSpec(memory_space=pltpu.VMEM),
            pl.BlockSpec(memory_space=pl.ANY),
            pl.BlockSpec(memory_space=pl.ANY),
        ],
        out_specs=pl.BlockSpec(memory_space=pltpu.VMEM),
        scratch_shapes=[
            pltpu.VMEM((query_rows, local_width), jnp.bfloat16),
            pltpu.VMEM((train_rows, local_width), jnp.bfloat16),
            pltpu.VMEM((2, query_rows, half), jnp.bfloat16),
            pltpu.VMEM((query_rows, PROJ), jnp.bfloat16),
            *swapped(query_rows, jnp.bfloat16),
            *swapped(train_rows, jnp.float32),
            pltpu.VMEM((PROJ, 128), jnp.float32),
            pltpu.VMEM((half, 128), jnp.float32),
            pltpu.VMEM((width, half), jnp.bfloat16),
            pltpu.VMEM((train_rows, half), jnp.bfloat16),
            pltpu.VMEM((width // QBLK, QBLK, train_rows), jnp.float32),
            pltpu.VMEM((out_width, train_rows), jnp.float32),
            pltpu.VMEM((out_width, train_rows), jnp.float32),
            pltpu.SemaphoreType.DMA((2,)),
            pltpu.SemaphoreType.DMA((4 + groups,)),
            pltpu.SemaphoreType.DMA((4 + groups,)),
            pltpu.SemaphoreType.DMA((outer * chunks,)),
            pltpu.SemaphoreType.DMA((outer * chunks,)),
            pltpu.SemaphoreType.DMA((2 * chunks,)),
            pltpu.SemaphoreType.DMA((max(1, (2 * outer - 1) * chunks * (inner - 1)),)),
            pltpu.SemaphoreType.DMA((ex_count * chunks,)),
        ],
        compiler_params=pltpu.CompilerParams(
            collective_id=0, has_side_effects=True, vmem_limit_bytes=60 * 1024 * 1024
        ),
        name="score_rows",
    )(column_order, pair_blocks.T, hadamard, sign_bits.reshape(1, local_width), query_sketch, train_sketch)


def body(ex_count, train_sketch, query_sketch, sign_bits, column_order, pair_blocks):
    hadamard = jnp.asarray(hadamard_table(HBLOCK))
    return score_rows(train_sketch, query_sketch, sign_bits, column_order, pair_blocks, hadamard, ex_count).T


def solution(mesh):
    placed = (
        P(("groups", "ex"), "wid"),
        P(("groups", "ex"), "wid"),
        P("wid"),
        P(),
        P("groups", None),
    )
    return jax.shard_map(
        functools.partial(body, mesh.shape["ex"]),
        mesh=mesh, in_specs=placed, out_specs=P(("groups", "ex"), None), check_vma=False,
    )
```
